512 devices in a mesh: seq: 64 (over z, y_lo, core), kv: 8 (over y_hi, x).
Axes of the slice: x: 4, y: 4 (y_hi: 2, y_lo: 2; y = y_hi * 2 + y_lo), z: 16, core: 2. Of those that a mesh axis runs over, the one named last changes fastest.
Arguments:
- queries: bfloat16 [8192, 8192], P('seq', 'kv'), parts along dimension 1, may hold values from -4.5 to 4.5
- keys: bfloat16 [8192, 1024], P('seq', 'kv'), parts along dimension 1, may hold values from -4.5 to 4.5
- values: bfloat16 [8192, 1024], P('seq', 'kv'), parts along dimension 1, may hold values from -6 to 6
- block_order: int32 [128], replicated, may hold values from 0 to 127, each once
Outputs:
- attention: bfloat16 [8192, 8192], P('seq', 'kv'), parts along dimension 1
- row_lse: float32 [64, 8192], P('kv', 'seq'), parts along dimension 0
- column_sums: float32 [65536], P(('kv', 'seq')), parts along dimension 0
The draws below stay inside these ranges and needn't reach their ends.
There are 8 independent parts, one for each index of `kv`. The reference program is written for one: setup_inputs(seed, part) draws one part's arguments, and reference() takes and returns one part's arrays. A program takes and returns all parts, laid end to end along the dimension named above; an argument that names none is the same for every part. Nothing has to cross between parts.
Inputs may be any that keep to these rules, and one draw needn't show every extreme that they name: `block_order`: every value of 0 to 127 appears once.
All inputs are finite; a program needn't handle non-finite values.
Results may differ from the reference program's by a relative error of at most 0.0047.
Values may be sent and summed in bfloat16 or wider, within the bound.
A program may use at most 64 MiB of HBM per device.

```python
import math
import jax
import jax.numpy as jnp
from jax import lax

HEADS = 8
HEAD_DIM = 128
BLOCK = 64
BLOCKS = 128
TOKENS = 8192


def base_values(key, shape):
    drawn = jax.random.normal(jax.random.fold_in(key, 6), shape, dtype=jnp.float32)
    return jnp.clip(drawn, -4.5, 4.5)


def draw_queries(key, part):
    drawn = base_values(jax.random.fold_in(key, 101), (TOKENS, HEADS * HEAD_DIM))
    return drawn.astype(jnp.bfloat16)


def draw_keys(key, part):
    drawn = base_values(jax.random.fold_in(key, 202), (TOKENS, HEAD_DIM))
    return drawn.astype(jnp.bfloat16)


def steps_of(stream_key, extent, shards, least, top_value):
    gain, own = 1.0, jax.random.fold_in(stream_key, 6)
    for axis_at, blocks in shards:
        draws = jnp.exp(jax.random.uniform(jax.random.fold_in(own, axis_at), (blocks,), jnp.float32, least / len(shards), top_value / len(shards)))
        gain = gain * jnp.repeat(draws, extent[axis_at] // blocks).reshape([-1 if axis == axis_at else 1 for axis in range(len(extent))])
    return gain


def scatter_about(rng, extent, scale, reach, split=(), kind=jnp.bfloat16):
    array = jax.random.normal(rng, extent, jnp.float32) * scale
    if len(split) > 0:
        array = steps_of(rng, extent, split, -0.22, 0.18) * array
    return jnp.clip(array, min=-reach, max=reach).astype(kind)


def setup_inputs(seed: int = 0, part: int = 0) -> dict:
    streams_of = jax.random.split(jax.random.key(seed), 5)
    part_keys = jax.random.split(jax.random.fold_in(streams_of[4], part), 5)
    queries = draw_queries(jax.random.fold_in(jax.random.fold_in(streams_of[4], part), 71), part)
    keys = draw_keys(jax.random.fold_in(jax.random.fold_in(streams_of[4], part), 71), part)
    values = scatter_about(part_keys[2], (TOKENS, HEAD_DIM), 1.0, 6.0, ((0, 64),))
    block_order = jax.random.permutation(streams_of[3], BLOCKS).astype(jnp.int32)
    return {"queries": queries, "keys": keys, "values": values, "block_order": block_order}


def reference(queries, keys, values, block_order):
    total_rows = keys.shape[0]
    head_dim = keys.shape[1]
    head_count = queries.shape[1] // head_dim
    row_ids = jnp.arange(total_rows, dtype=jnp.int32)
    positions = (block_order[row_ids // BLOCK] * BLOCK + row_ids % BLOCK).astype(jnp.int32)
    query_all = queries.astype(jnp.float32).reshape(total_rows, head_count, head_dim)
    key_all = keys.astype(jnp.float32)
    value_all = values.astype(jnp.float32)
    width = math.gcd(total_rows, 512)
    turns = total_rows // width
    factor = 1.0 / math.sqrt(head_dim)

    def one_block(columns, block_index):
        first = (block_index * width).astype(jnp.int32)
        query_tile = lax.dynamic_slice_in_dim(query_all, first, width, 0)
        query_pos = lax.dynamic_slice_in_dim(positions, first, width, 0)
        scores = jnp.einsum('qhd,kd->hqk', query_tile, key_all) * factor
        allowed = positions[None, :] <= query_pos[:, None]
        scores = jnp.where(allowed[None, :, :], scores, -jnp.inf)
        top = lax.optimization_barrier(jnp.max(scores, axis=2))
        lse_tile = top + jnp.log(lax.optimization_barrier(jnp.sum(jnp.exp(scores - top[:, :, None]), axis=2)))
        probs = jnp.exp(scores - lse_tile[:, :, None])
        columns = columns + lax.optimization_barrier(jnp.sum(probs, axis=(0, 1)))
        weights = lax.optimization_barrier(probs.astype(jnp.bfloat16)).astype(jnp.float32)
        output = jnp.einsum('hqk,kd->qhd', weights, value_all).reshape(width, head_count * head_dim).astype(jnp.bfloat16)
        return (columns, (output, lse_tile))
    columns, (outputs, lse_all) = lax.scan(one_block, jnp.zeros((total_rows,), jnp.float32), jnp.arange(turns, dtype=jnp.int32))
    attention = outputs.reshape(total_rows, head_count * head_dim)
    row_lse = jnp.transpose(lse_all, (1, 0, 2)).reshape(head_count, total_rows)
    return (attention, row_lse, columns)
```

```python
import functools
import math

import jax
import jax.numpy as jnp
from jax import lax
from jax.experimental import pallas as pl
from jax.experimental.pallas import tpu as pltpu
from jax.sharding import PartitionSpec as P

MESH = pl.DeviceIdType.MESH
F32, BF16 = jnp.float32, jnp.bfloat16
BLOCK = 64
ROWS = 128
DIM = 128
HEADS = 8
Z = 16
TILE = 256
NEG = -1e30
LOG2E = math.log2(math.e)
SCALE = LOG2E / math.sqrt(DIM)
KEYS = Z * 2 * ROWS
CHUNKS = [(0, 256)] + [(256 + 512 * (d - 1), 512) for d in range(1, 8)] + [(3840, 256)]


def place(rho):
    rho %= Z
    return 2 * rho - 1 if 1 <= rho <= 8 else (2 * (Z - rho)) % (2 * Z)


def slot(rho, other):
    return 2 * place(rho) + other


def copies_from(rho, other):
    rho %= Z
    out = []
    if other == 0:
        if rho == 0:
            return [(3, 0, 0, ROWS), (-3, 0, 0, ROWS), (0, 1, 0, ROWS), (1, 0, 0, ROWS), (-1, 0, 0, ROWS)]
        if rho == 13:
            out = [(3, 0, 0, ROWS), (1, 0, 0, ROWS), (-1, 0, 0, ROWS)]
        if rho == 3:
            out = [(-3, 0, 0, ROWS), (-1, 0, 0, ROWS), (1, 0, 0, ROWS)]
        if rho not in (5, 7, 8, 9, 11):
            out.insert(1, (0, 1, 0, ROWS))
    if rho == 10:
        out += [(2, 0, 0, 64), (1, 0, 0, ROWS), (-1, 0, 0, ROWS)]
    if rho == 6:
        out += [(-2, 0, 64, 64), (-1, 0, 0, ROWS), (1, 0, 0, ROWS)]
    return out


def all_copies():
    number, arrivals = {}, {}
    for rho in range(Z):
        for other in (0, 1):
            for dz, dy, lo, rows in copies_from(rho, other):
                key = (rho, other, dz, dy)
                number[key] = len(number)
                target = ((rho - dz) % Z, other ^ dy)
                arrivals.setdefault(target, []).append((number[key], lo, rows))
    return number, arrivals


NUMBER, ARRIVALS = all_copies()
COPIES = len(NUMBER)
SEM_COL = 2 * COPIES
SEM_Q = SEM_COL + 32
SEM_LSE = SEM_Q + 1
SEM_OUT = SEM_LSE + 1
SEMS = SEM_OUT + 4


def dot_nt(a, b):
    return lax.dot_general(a, b, (((1,), (1,)), ((), ())), preferred_element_type=F32)


def iota(shape, axis):
    return lax.broadcasted_iota(jnp.int32, shape, axis)


def kernel(
    q_ref, k_ref, v_ref, order_ref, att_ref, lse_ref, col_ref,
    kbuf, vbuf, qd, qb, hot, ex, m_s, l_s, f_s, ot, vt, cs, csr, lpart, lrecv, obuf, orecv, send, recv,
):
    me = lax.axis_index("seq")
    z, y, c = me // 4, (me // 2) % 2, me % 2

    def device(dz, dy, dc):
        zz = lax.rem(z + dz + Z, Z)
        yy = 1 - y if dy else y
        cc = 1 - c if dc else c
        return {"seq": zz * 4 + yy * 2 + cc}

    barrier = pltpu.get_barrier_semaphore()
    partners = [(d, 0, 0) for d in (-3, -2, -1, 1, 2, 3)] + [(0, 1, 0), (0, 0, 1)]
    for p in partners:
        pl.semaphore_signal(barrier, inc=1, device_id=device(*p), device_id_type=MESH)

    def remote(src, dst, index, target):
        return pltpu.make_async_remote_copy(
            src_ref=src, dst_ref=dst, send_sem=send.at[index], recv_sem=recv.at[index],
            device_id=target, device_id_type=MESH,
        )

    bufs = (kbuf, vbuf)
    pending = []

    def block_copy(a, rho, other, dz, dy, lo, rows):
        src = slot(rho, other) * ROWS + lo
        dst = slot(rho - dz, other ^ dy) * ROWS + lo
        return remote(
            bufs[a].at[pl.ds(src, rows)], bufs[a].at[pl.ds(dst, rows)],
            a * COPIES + NUMBER[(rho % Z, other, dz, dy)], device(dz, dy, 0),
        )

    def forward(a, rho, other):
        for dz, dy, lo, rows in copies_from(rho, other):
            cp = block_copy(a, rho, other, dz, dy, lo, rows)
            cp.start()
            pending.append(cp)

    waited = set()

    def arrive(a, rho, other, then_forward=True):
        rho %= Z
        if (a, rho, other) in waited:
            return
        waited.add((a, rho, other))
        for index, lo, rows in ARRIVALS[(rho, other)]:
            here = bufs[a].at[pl.ds(slot(rho, other) * ROWS + lo, rows)]
            remote(here, here, a * COPIES + index, device(0, 1, 0)).wait_recv()
        if then_forward:
            forward(a, rho, other)

    kbuf[0:ROWS, :] = k_ref[...]
    vbuf[0:ROWS, :] = v_ref[...]
    for h in range(HEADS):
        part = q_ref[:, h * DIM:(h + 1) * DIM].astype(F32)
        qd[h // 2, :, (h % 2) * ROWS:(h % 2 + 1) * ROWS] = jnp.transpose(part).astype(BF16)

    order = order_ref[...]
    row = iota((128, 128), 0)
    lane = iota((128, 128), 1)
    at = row // 4
    rho = jnp.where(at % 2 == 1, (at + 1) // 2, Z - at // 2)
    src_z = (z + rho) % Z
    src_y = jnp.where((row // 2) % 2 == 1, 1 - y, y)
    index = 2 * (src_z * 4 + src_y * 2 + c) + row % 2
    key_block = jnp.sum(jnp.where(lane == index, order, 0), axis=1, keepdims=True)
    half = (iota((1, TILE), 1) % ROWS) // BLOCK
    lane1 = iota((1, 128), 1)
    for dc in (0, 1):
        first = 2 * (z * 4 + y * 2 + (1 - c if dc else c))
        b0 = jnp.sum(jnp.where(lane1 == first, order, 0), axis=1, keepdims=True)
        b1 = jnp.sum(jnp.where(lane1 == first + 1, order, 0), axis=1, keepdims=True)
        query_block = jnp.where(half == 0, b0, b1)
        bad = (key_block > query_block) & (iota((128, TILE), 0) < 64)
        bias = jnp.where(bad, NEG, 0.0).astype(BF16)
        for t in range(4):
            qb[4 * dc + t] = bias
    for r in range(0, KEYS, 512):
        hot[r:r + 512, :] = jnp.where(
            iota((512, 128), 1) == (iota((512, 128), 0) + r) // BLOCK, 1.0, 0.0
        ).astype(BF16)
    kr, qr = iota((ROWS, TILE), 0), iota((ROWS, TILE), 1) % ROWS
    tri = jnp.where((kr // BLOCK == qr // BLOCK) & (kr > qr), NEG, 0.0)

    def scores(ci):
        lo, n = CHUNKS[ci]

        def tile(t, masked):
            lhs = jnp.concatenate([kbuf[lo:lo + n, :], hot[lo:lo + n, :]], axis=1)
            rhs = jnp.concatenate([qd[t], qb[t]], axis=0)
            s = jnp.dot(lhs, rhs, preferred_element_type=F32)
            if masked:
                s = jnp.concatenate([s[:ROWS] + tri, s[ROWS:]], axis=0)
            top = jnp.max(s, axis=0, keepdims=True) * SCALE
            p = jnp.exp2(s * SCALE - top)
            m_s[ci, t] = top
            l_s[ci, t] = jnp.sum(p, axis=0, keepdims=True)
            ex[t, lo:lo + n, :] = p.astype(BF16)

        @pl.loop(0, 4)
        def _(t):
            tile(t, ci == 0)

        @pl.loop(4, 8)
        def _(t):
            tile(t, False)

    def column(ci):
        lo, n = CHUNKS[ci]
        pick = iota((16, TILE), 0)
        total = jnp.zeros((16, n), F32)
        for t in range(8):
            f = f_s[ci, t]
            high = f.astype(BF16).astype(F32)
            w = jnp.where(pick == 0, high, jnp.where(pick == 1, f - high, 0.0)).astype(BF16)
            total = total + dot_nt(w, ex[t, lo:lo + n, :])
        total = total[0:1] + total[1:2]
        for b in range(n // ROWS):
            cs[lo // ROWS + b] = total[:, b * ROWS:(b + 1) * ROWS]

    def send_column(rho, other):
        here, there = slot(rho, other), slot(-rho, other)
        cp = remote(cs.at[here], csr.at[there], SEM_COL + there, device(rho % Z, other, 0))
        cp.start()
        pending.append(cp)

    def mix(ci, start):
        lo, n = CHUNKS[ci]
        vt[:, 0:n] = jnp.transpose(vbuf[lo:lo + n, :].astype(F32)).astype(BF16)

        @pl.loop(0, 8)
        def _(t):
            o = jnp.dot(vt[:, 0:n], ex[t, lo:lo + n, :], preferred_element_type=F32) * f_s[ci, t]
            if start:
                ot[t] = o
            else:
                ot[t] += o

    pl.semaphore_wait(barrier, len(partners))

    forward(0, 0, 0)
    q_copy = remote(qd.at[pl.ds(0, 4)], qd.at[pl.ds(4, 4)], SEM_Q, device(0, 0, 1))
    q_copy.start()
    forward(1, 0, 0)

    def both(a, d, other):
        arrive(a, d, other)
        arrive(a, -d, other)

    q_copy.wait_recv()
    arrive(0, 0, 1)
    scores(0)
    both(0, 3, 0)
    both(0, 1, 0)
    both(0, 1, 1)
    scores(1)
    both(1, 3, 0)
    both(1, 1, 0)
    both(0, 3, 1)
    both(0, 6, 0)
    both(0, 4, 0)
    both(0, 2, 0)
    scores(3)
    both(0, 6, 1)
    both(1, 6, 0)
    both(0, 2, 1)
    scores(2)
    both(1, 4, 0)
    both(1, 2, 0)
    scores(6)
    both(0, 4, 1)
    scores(4)
    both(1, 6, 1)
    both(0, 5, 0)
    both(0, 5, 1)
    scores(5)
    both(0, 7, 0)
    both(0, 7, 1)
    scores(7)
    arrive(0, 8, 0)
    arrive(0, 8, 1)
    scores(8)

    top = m_s[0]
    for ci in range(1, 9):
        top = jnp.maximum(top, m_s[ci])
    total = l_s[0] * jnp.exp2(m_s[0] - top)
    for ci in range(1, 9):
        total = total + l_s[ci] * jnp.exp2(m_s[ci] - top)
    lpart[...] = top + jnp.log(total) * LOG2E
    l_copy = remote(lpart, lrecv, SEM_LSE, device(0, 0, 1))
    l_copy.start()
    l_copy.wait_recv()
    for t in range(8):
        a, b = lpart[t], lrecv[(t + 4) % 8]
        top = jnp.maximum(a, b)
        lse = top + jnp.log(jnp.exp2(a - top) + jnp.exp2(b - top)) * LOG2E
        for ci in range(9):
            f_s[ci, t] = jnp.exp2(m_s[ci, t] - lse)
        if t < 4:
            for h in range(2):
                lse_ref[2 * t + h:2 * t + h + 1, :] = lse[:, h * ROWS:(h + 1) * ROWS] / LOG2E

    for ci in range(8, -1, -1):
        column(ci)
        for d in ((ci,) if ci in (0, 8) else (ci, -ci)):
            for other in (0, 1):
                if (d, other) != (0, 0):
                    send_column(d, other)

    for step, ci in enumerate((0, 1, 3, 2, 4, 6, 5, 7, 8)):
        for d in ((ci,) if ci in (0, 8) else (ci, -ci)):
            for other in (0, 1):
                if (d, other) != (0, 0):
                    arrive(1, d, other)
        mix(ci, step == 0)

    out_copies = []
    for t in range(4):
        obuf[t] = ot[4 + t].astype(BF16)
        cp = remote(obuf.at[t], orecv.at[t], SEM_OUT + t, device(0, 0, 1))
        cp.start()
        out_copies.append(cp)
    for t in range(4):
        out_copies[t].wait_recv()
        o = ot[t] + orecv[t].astype(F32)
        for h in range(2):
            at = (2 * t + h) * DIM
            att_ref[:, at:at + DIM] = jnp.transpose(o[:, h * ROWS:(h + 1) * ROWS]).astype(BF16)

    total = cs[0]
    for s in range(1, 32):
        remote(cs.at[s], csr.at[s], SEM_COL + s, device(0, 1, 0)).wait_recv()
        total = total + csr[s]
    col_ref[...] = total
    for cp in pending + [q_copy, l_copy] + out_copies:
        cp.wait_send()


def local(queries, keys, values, block_order):
    vmem = pl.BlockSpec(memory_space=pltpu.VMEM)
    attention, row_lse, columns = pl.pallas_call(
        kernel,
        out_shape=(
            jax.ShapeDtypeStruct((ROWS, HEADS * DIM), BF16),
            jax.ShapeDtypeStruct((HEADS, ROWS), F32),
            jax.ShapeDtypeStruct((1, ROWS), F32),
        ),
        in_specs=[vmem] * 4,
        out_specs=(vmem,) * 3,
        scratch_shapes=[
            pltpu.VMEM((KEYS, DIM), BF16),
            pltpu.VMEM((KEYS, DIM), BF16),
            pltpu.VMEM((8, DIM, TILE), BF16),
            pltpu.VMEM((8, 128, TILE), BF16),
            pltpu.VMEM((KEYS, 128), BF16),
            pltpu.VMEM((8, KEYS, TILE), BF16),
            pltpu.VMEM((9, 8, 1, TILE), F32),
            pltpu.VMEM((9, 8, 1, TILE), F32),
            pltpu.VMEM((9, 8, 1, TILE), F32),
            pltpu.VMEM((8, DIM, TILE), F32),
            pltpu.VMEM((DIM, 512), BF16),
            pltpu.VMEM((32, 1, ROWS), F32),
            pltpu.VMEM((32, 1, ROWS), F32),
            pltpu.VMEM((8, 1, TILE), F32),
            pltpu.VMEM((8, 1, TILE), F32),
            pltpu.VMEM((4, DIM, TILE), BF16),
            pltpu.VMEM((4, DIM, TILE), BF16),
            pltpu.SemaphoreType.DMA((SEMS,)),
            pltpu.SemaphoreType.DMA((SEMS,)),
        ],
        compiler_params=pltpu.CompilerParams(
            collective_id=0, has_side_effects=True, vmem_limit_bytes=52 * 2**20
        ),
        cost_estimate=pl.CostEstimate(flops=9 * 10**9, bytes_accessed=10**6, transcendentals=9 * 10**6),
    )(queries, keys, values, block_order.reshape(1, -1))
    return attention, row_lse, columns.reshape(ROWS)


def solution(mesh):
    placed = (P("seq", "kv"), P("seq", "kv"), P("seq", "kv"), P())
    return jax.shard_map(
        local,
        mesh=mesh,
        in_specs=placed,
        out_specs=(P("seq", "kv"), P("kv", "seq"), P(("kv", "seq"))),
        check_vma=False,
    )
```

```python
import functools
import math

import jax
import jax.numpy as jnp
from jax import lax
from jax.experimental import pallas as pl
from jax.experimental.pallas import tpu as pltpu
from jax.sharding import PartitionSpec as P

MESH = pl.DeviceIdType.MESH
F32, BF16 = jnp.float32, jnp.bfloat16
BLOCK = 64
ROWS = 128
DIM = 128
HEADS = 8
Z = 16
TILE = 256
TILES = 16
NEG = -1e30
LOG2E = math.log2(math.e)
SCALE = LOG2E / math.sqrt(DIM)
KEYS = Z * ROWS
GROUPS = [(0, 1, -1), (3, -3), (2, -2, 4, -4), (6, -6), (5, -5), (7, -7, 8)]
ORDER = [rho for group in GROUPS for rho in group]
CHUNKS = []
for group in GROUPS:
    CHUNKS.append((sum(n for _, n in CHUNKS), ROWS * len(group)))
NC = len(CHUNKS)
PLACE = {rho % Z: at for at, rho in enumerate(ORDER)}


def slot(rho):
    return PLACE[rho % Z]


COPIES_FROM = {
    0: [(3, 0, ROWS), (-3, 0, ROWS), (1, 0, ROWS), (-1, 0, ROWS)],
    -3: [(3, 0, ROWS), (1, 0, ROWS), (-1, 0, ROWS)],
    3: [(-3, 0, ROWS), (-1, 0, ROWS), (1, 0, ROWS)],
    -6: [(2, 0, 64), (1, 0, ROWS), (-1, 0, ROWS)],
    6: [(-2, 64, 64), (-1, 0, ROWS), (1, 0, ROWS)],
}
NUMBER, ARRIVALS = {}, {}
for rho, copies in COPIES_FROM.items():
    for dz, lo, rows in copies:
        NUMBER[rho, dz] = len(NUMBER)
        ARRIVALS.setdefault((rho - dz) % Z, []).append((NUMBER[rho, dz], lo, rows))
COPIES = len(NUMBER)
SEM_COL = 2 * COPIES
SEM_Q = SEM_COL + Z
SEM_LSE = SEM_Q + 3
SEM_OUT = SEM_LSE + 3
SEMS = SEM_OUT + 12

EVENTS = [
    ("K", 3), ("K", 1), ("Q", 1), ("S", 0, 0), ("S", 0, 1), ("S", 1, 0), ("S", 1, 1), ("V", 3),
    ("Q", 2), ("S", 0, 2), ("S", 1, 2), ("K", 6), ("V", 1), ("Q", 3), ("S", 0, 3), ("S", 1, 3),
    ("K", 2), ("K", 4), ("S", 2, 0), ("S", 2, 1), ("V", 6), ("S", 2, 2), ("S", 2, 3),
    ("S", 3, 0), ("S", 3, 1), ("S", 3, 2), ("S", 3, 3),
    ("K", 5), ("S", 4, 0), ("S", 4, 1), ("S", 4, 2), ("S", 4, 3),
    ("K", 7), ("K", 8), ("S", 5, 0), ("S", 5, 1), ("S", 5, 2), ("S", 5, 3),
]

V_LAST = (2, 4, 5, 7, 8)
COLUMN_ORDER = (5, 3, 4, 2, 1, 0)


def dot_nt(a, b):
    return lax.dot_general(a, b, (((1,), (1,)), ((), ())), preferred_element_type=F32)


def add_log(a, b):
    top = jnp.maximum(a, b)
    return top + jnp.log(jnp.exp2(a - top) + jnp.exp2(b - top)) * LOG2E


def iota(shape, axis):
    return lax.broadcasted_iota(jnp.int32, shape, axis)


def kernel(
    q_hbm, k_hbm, v_hbm, order_hbm, att_ref, lse_ref, col_ref,
    qin, order_ref, kbuf, vbuf, qd, qb, hot, ex, m_s, l_s, f_s, ot, vt, cs, csr, lpart, lrecv, share,
    obuf, orecv, osum, load, send, recv,
):
    me = lax.axis_index("seq")
    z, y, c = me // 4, (me // 2) % 2, me % 2

    def device(dz, dy, dc):
        zz = lax.rem(z + dz + Z, Z)
        yy = 1 - y if dy else y
        cc = 1 - c if dc else c
        return {"seq": zz * 4 + yy * 2 + cc}

    barrier = pltpu.get_barrier_semaphore()
    partners = [(d, 0, 0) for d in (-3, -2, -1, 1, 2, 3)] + [(0, 0, 1), (0, 1, 0), (0, 1, 1)]
    for p in partners:
        pl.semaphore_signal(barrier, inc=1, device_id=device(*p), device_id_type=MESH)

    loads = [
        pltpu.make_async_copy(q_hbm, qin, load.at[0]),
        pltpu.make_async_copy(k_hbm, kbuf.at[pl.ds(0, ROWS)], load.at[1]),
        pltpu.make_async_copy(v_hbm, vbuf.at[pl.ds(0, ROWS)], load.at[2]),
        pltpu.make_async_copy(order_hbm, order_ref, load.at[3]),
    ]
    for cp in loads:
        cp.start()

    pending = []

    def remote(src, dst, index, target):
        return pltpu.make_async_remote_copy(
            src_ref=src, dst_ref=dst, send_sem=send.at[index], recv_sem=recv.at[index],
            device_id=target, device_id_type=MESH,
        )

    def push(*args):
        cp = remote(*args)
        cp.start()
        pending.append(cp)

    bufs = (kbuf, vbuf)

    def forward(a, rho):
        for dz, lo, rows in COPIES_FROM.get(rho, ()):
            push(
                bufs[a].at[pl.ds(slot(rho) * ROWS + lo, rows)],
                bufs[a].at[pl.ds(slot(rho - dz) * ROWS + lo, rows)],
                a * COPIES + NUMBER[rho, dz], device(dz, 0, 0),
            )

    def arrive(a, rho):
        for index, lo, rows in ARRIVALS[rho % Z]:
            here = bufs[a].at[pl.ds(slot(rho) * ROWS + lo, rows)]
            remote(here, here, a * COPIES + index, device(1, 0, 0)).wait_recv()
        forward(a, rho)

    for r in range(0, KEYS, 512):
        hot[r:r + 512, :] = jnp.where(
            iota((512, 128), 1) == (iota((512, 128), 0) + r) // BLOCK, 1.0, 0.0
        ).astype(BF16)
    row, lane, lane1 = iota((128, 128), 0), iota((128, 128), 1), iota((1, 128), 1)
    rho = jnp.zeros((128, 128), jnp.int32)
    for at, value in enumerate(ORDER):
        rho = jnp.where(row // 2 == at, value % Z, rho)
    index = 2 * (((z + rho) % Z) * 4 + y * 2 + c) + row % 2
    kr, qr = iota((ROWS, TILE), 0), iota((ROWS, TILE), 1) % ROWS
    tri = jnp.where((kr // BLOCK == qr // BLOCK) & (kr > qr), NEG, 0.0)
    half = (iota((1, TILE), 1) % ROWS) // BLOCK
    loads[3].wait()
    order = order_ref[...]
    key_block = jnp.sum(jnp.where(lane == index, order, 0), axis=1, keepdims=True)
    for g in range(4):
        yy = 1 - y if g // 2 else y
        cc = 1 - c if g % 2 else c
        first = 2 * (z * 4 + yy * 2 + cc)
        b0 = jnp.sum(jnp.where(lane1 == first, order, 0), axis=1, keepdims=True)
        b1 = jnp.sum(jnp.where(lane1 == first + 1, order, 0), axis=1, keepdims=True)
        query_block = jnp.where(half == 0, b0, b1)
        bad = (key_block > query_block) & (iota((128, TILE), 0) < 2 * Z)
        qb[g] = jnp.where(bad, NEG, 0.0).astype(BF16)
    loads[0].wait()
    for h in range(HEADS):
        part = qin[:, h * DIM:(h + 1) * DIM].astype(F32)
        qd[h // 2, :, (h % 2) * ROWS:(h % 2 + 1) * ROWS] = jnp.transpose(part).astype(BF16)
    loads[1].wait()
    loads[2].wait()

    def scores(ci, g):
        lo, n = CHUNKS[ci]
        for t in range(4 * g, 4 * g + 4):
            lhs = jnp.concatenate([kbuf[lo:lo + n, :], hot[lo:lo + n, :]], axis=1)
            rhs = jnp.concatenate([qd[t], qb[g]], axis=0)
            s = jnp.dot(lhs, rhs, preferred_element_type=F32)
            if ci == 0 and g == 0:
                s = jnp.concatenate([s[:ROWS] + tri, s[ROWS:]], axis=0)
            top = jnp.max(s, axis=0, keepdims=True) * SCALE
            p = jnp.exp2(s * SCALE - top)
            m_s[ci, t] = top
            l_s[ci, t] = jnp.sum(p, axis=0, keepdims=True)
            ex[t, lo:lo + n, :] = p.astype(BF16)

    def column(ci):
        lo, n = CHUNKS[ci]
        pick = iota((16, TILE), 0)
        total = jnp.zeros((16, n), F32)
        for t in range(TILES):
            f = f_s[ci, t]
            high = f.astype(BF16).astype(F32)
            w = jnp.where(pick == 0, high, jnp.where(pick == 1, f - high, 0.0)).astype(BF16)
            total = total + dot_nt(w, ex[t, lo:lo + n, :])
        total = total[0:1] + total[1:2]
        for b in range(n // ROWS):
            cs[lo // ROWS + b] = total[:, b * ROWS:(b + 1) * ROWS]
        for rho in GROUPS[ci]:
            if rho:
                push(cs.at[slot(rho)], csr.at[slot(-rho)], SEM_COL + slot(-rho), device(rho % Z, 0, 0))

    def mix(t):
        total = None
        for ci, (lo, n) in enumerate(CHUNKS):
            o = jnp.dot(vt[:, lo:lo + n], ex[t, lo:lo + n, :], preferred_element_type=F32)
            o = o * jnp.exp2(m_s[ci, t] - lpart[t])
            total = o if total is None else total + o
        return total

    queries = [
        remote(qd.at[pl.ds(0, 4)], qd.at[pl.ds(4, 4)], SEM_Q, device(0, 0, 1)),
        remote(qd.at[pl.ds(0, 4)], qd.at[pl.ds(8, 4)], SEM_Q + 1, device(0, 1, 0)),
        remote(qd.at[pl.ds(8, 4)], qd.at[pl.ds(12, 4)], SEM_Q + 2, device(0, 0, 1)),
    ]
    pending.extend(queries)

    pl.semaphore_wait(barrier, len(partners))

    forward(0, 0)
    queries[1].start()
    queries[0].start()
    forward(1, 0)
    for what, *at in EVENTS:
        if what == "S":
            scores(*at)
        elif what == "Q":
            queries[at[0] - 1].wait_recv()
            if at[0] == 2:
                queries[2].start()
        else:
            arrive("KV".index(what), at[0])
            if at[0] != 8:
                arrive("KV".index(what), -at[0])

    for t in range(TILES):
        top = m_s[0, t]
        for ci in range(1, NC):
            top = jnp.maximum(top, m_s[ci, t])
        total = l_s[0, t] * jnp.exp2(m_s[0, t] - top)
        for ci in range(1, NC):
            total = total + l_s[ci, t] * jnp.exp2(m_s[ci, t] - top)
        lpart[t] = top + jnp.log(total) * LOG2E
    lses = [remote(lpart, lrecv.at[g - 1], SEM_LSE + g - 1, device(0, g // 2, g % 2)) for g in (3, 2, 1)]
    for cp in lses:
        cp.start()
    pending.extend(lses)
    for rho in V_LAST:
        arrive(1, rho)
        if rho != 8:
            arrive(1, -rho)
    for ci, (lo, n) in enumerate(CHUNKS):
        vt[:, lo:lo + n] = jnp.transpose(vbuf[lo:lo + n, :].astype(F32)).astype(BF16)

    def out_copy(kind, t):
        src = (obuf.at[t], obuf.at[4 + t], osum.at[t])[kind]
        return remote(src, orecv.at[4 * kind + t], SEM_OUT + 4 * kind + t, device(0, *((0, 1), (0, 1), (1, 0))[kind]))

    outs = [[out_copy(kind, t) for t in range(4)] for kind in range(3)]
    for t in range(4):
        obuf[t] = mix(12 + t).astype(BF16)
        outs[0][t].start()
    for t in range(4):
        ot[t] = mix(8 + t)
    lses[2].wait_recv()
    for t in range(4):
        a, b = lpart[8 + t], lrecv[0, 12 + t]
        two = add_log(a, b)
        outs[0][t].wait_recv()
        osum[t] = (ot[t] * jnp.exp2(a - two) + orecv[t].astype(F32) * jnp.exp2(b - two)).astype(BF16)
        outs[2][t].start()
    for t in range(4):
        obuf[4 + t] = mix(4 + t).astype(BF16)
        outs[1][t].start()
    lses[1].wait_recv()
    lses[0].wait_recv()
    for t in range(TILES):
        g = t // 4
        parts = [lpart[t]] + [lrecv[o - 1, (o ^ g) * 4 + t % 4] for o in (1, 2, 3)]
        pair = add_log(parts[2], parts[3])
        lse = add_log(add_log(parts[0], parts[1]), pair)
        for ci in range(NC):
            f_s[ci, t] = jnp.exp2(m_s[ci, t] - lse)
        if t < 4:
            share[0, t] = jnp.exp2(parts[0] - lse)
            share[1, t] = jnp.exp2(parts[1] - lse)
            share[2, t] = jnp.exp2(pair - lse)
            for h in range(2):
                lse_ref[2 * t + h:2 * t + h + 1, :] = lse[:, h * ROWS:(h + 1) * ROWS] / LOG2E
    for ci in COLUMN_ORDER:
        column(ci)
    for t in range(4):
        ot[t] = mix(t)
    for t in range(4):
        outs[1][t].wait_recv()
        outs[2][t].wait_recv()
        o = (
            ot[t] * share[0, t] + orecv[4 + t].astype(F32) * share[1, t] + orecv[8 + t].astype(F32) * share[2, t]
        )
        for h in range(2):
            at = (2 * t + h) * DIM
            att_ref[:, at:at + DIM] = jnp.transpose(o[:, h * ROWS:(h + 1) * ROWS]).astype(BF16)

    total = cs[0]
    for s in range(1, Z):
        remote(cs.at[s], csr.at[s], SEM_COL + s, device(1, 0, 0)).wait_recv()
        total = total + csr[s]
    col_ref[...] = total
    for cp in pending + outs[0] + outs[1] + outs[2]:
        cp.wait_send()


def local(queries, keys, values, block_order):
    vmem = pl.BlockSpec(memory_space=pltpu.VMEM)
    hbm = pl.BlockSpec(memory_space=pltpu.HBM)
    attention, row_lse, columns = pl.pallas_call(
        kernel,
        out_shape=(
            jax.ShapeDtypeStruct((ROWS, HEADS * DIM), BF16),
            jax.ShapeDtypeStruct((HEADS, ROWS), F32),
            jax.ShapeDtypeStruct((1, ROWS), F32),
        ),
        in_specs=[hbm] * 4,
        out_specs=(vmem,) * 3,
        scratch_shapes=[
            pltpu.VMEM((ROWS, HEADS * DIM), BF16),
            pltpu.VMEM((1, 128), jnp.int32),
            pltpu.VMEM((KEYS, DIM), BF16),
            pltpu.VMEM((KEYS, DIM), BF16),
            pltpu.VMEM((TILES, DIM, TILE), BF16),
            pltpu.VMEM((4, 128, TILE), BF16),
            pltpu.VMEM((KEYS, 128), BF16),
            pltpu.VMEM((TILES, KEYS, TILE), BF16),
            pltpu.VMEM((NC, TILES, 1, TILE), F32),
            pltpu.VMEM((NC, TILES, 1, TILE), F32),
            pltpu.VMEM((NC, TILES, 1, TILE), F32),
            pltpu.VMEM((4, DIM, TILE), F32),
            pltpu.VMEM((DIM, KEYS), BF16),
            pltpu.VMEM((Z, 1, ROWS), F32),
            pltpu.VMEM((Z, 1, ROWS), F32),
            pltpu.VMEM((TILES, 1, TILE), F32),
            pltpu.VMEM((3, TILES, 1, TILE), F32),
            pltpu.VMEM((3, 4, 1, TILE), F32),
            pltpu.VMEM((8, DIM, TILE), BF16),
            pltpu.VMEM((12, DIM, TILE), BF16),
            pltpu.VMEM((4, DIM, TILE), BF16),
            pltpu.SemaphoreType.DMA((4,)),
            pltpu.SemaphoreType.DMA((SEMS,)),
            pltpu.SemaphoreType.DMA((SEMS,)),
        ],
        compiler_params=pltpu.CompilerParams(
            collective_id=0, has_side_effects=True, vmem_limit_bytes=63 * 2**20
        ),
        cost_estimate=pl.CostEstimate(flops=9 * 10**9, bytes_accessed=10**6, transcendentals=9 * 10**6),
    )(queries, keys, values, block_order.reshape(1, -1))
    return attention, row_lse, columns.reshape(ROWS)


def solution(mesh):
    placed = (P("seq", "kv"), P("seq", "kv"), P("seq", "kv"), P())
    return jax.shard_map(
        local,
        mesh=mesh,
        in_specs=placed,
        out_specs=(P("seq", "kv"), P("kv", "seq"), P(("kv", "seq"))),
        check_vma=False,
    )
```

```python
import functools
import math

import jax
import jax.numpy as jnp
from jax import lax
from jax.experimental import pallas as pl
from jax.experimental.pallas import tpu as pltpu
from jax.sharding import PartitionSpec as P

MESH = pl.DeviceIdType.MESH
F32, BF16 = jnp.float32, jnp.bfloat16
BLOCK = 64
ROWS = 128
DIM = 128
HEADS = 8
Z = 16
TILE = 256
TILES = 16
NEG = -1e30
LOG2E = math.log2(math.e)
SCALE = LOG2E / math.sqrt(DIM)
KEYS = Z * ROWS
GROUPS = [(0, 1, -1), (3, -3), (2, -2, 4, -4), (6, -6), (5, -5), (7, -7, 8)]
ORDER = [rho for group in GROUPS for rho in group]
CHUNKS = []
for group in GROUPS:
    CHUNKS.append((sum(n for _, n in CHUNKS), ROWS * len(group)))
NC = len(CHUNKS)
PLACE = {rho % Z: at for at, rho in enumerate(ORDER)}


def slot(rho):
    return PLACE[rho % Z]


COPIES_FROM = {
    0: [(3, 0, ROWS), (-3, 0, ROWS), (1, 0, ROWS), (-1, 0, ROWS)],
    -3: [(3, 0, ROWS), (1, 0, ROWS), (-1, 0, ROWS)],
    3: [(-3, 0, ROWS), (-1, 0, ROWS), (1, 0, ROWS)],
    -6: [(2, 0, 64), (1, 0, ROWS), (-1, 0, ROWS)],
    6: [(-2, 64, 64), (-1, 0, ROWS), (1, 0, ROWS)],
}
NUMBER, ARRIVALS = {}, {}
for rho, copies in COPIES_FROM.items():
    for dz, lo, rows in copies:
        NUMBER[rho, dz] = len(NUMBER)
        ARRIVALS.setdefault((rho - dz) % Z, []).append((NUMBER[rho, dz], lo, rows))
COPIES = len(NUMBER)
SEM_COL = 2 * COPIES
SEM_Q = SEM_COL + Z
SEM_LSE = SEM_Q + 3
SEM_OUT = SEM_LSE + 3
SEMS = SEM_OUT + 12

EVENTS = [
    ("K", 3), ("K", 1), ("Q", 1), ("S", 0, 0), ("S", 0, 1), ("S", 1, 0), ("S", 1, 1), ("V", 3),
    ("Q", 2), ("S", 0, 2), ("S", 1, 2), ("K", 6), ("V", 1), ("Q", 3), ("S", 0, 3), ("S", 1, 3),
    ("K", 2), ("K", 4), ("S", 2, 0), ("S", 2, 1), ("V", 6), ("S", 2, 2), ("S", 2, 3),
    ("S", 3, 0), ("S", 3, 1), ("S", 3, 2), ("S", 3, 3),
    ("K", 5), ("S", 4, 0), ("S", 4, 1), ("S", 4, 2), ("S", 4, 3),
    ("K", 7), ("K", 8), ("S", 5, 0), ("S", 5, 1), ("S", 5, 2), ("S", 5, 3),
]

DOT_TILES = 8
V_LAST = (2, 4, 5, 7, 8)
COLUMN_ORDER = (5, 3, 4, 2, 1, 0)


def dot_nt(a, b):
    return lax.dot_general(a, b, (((1,), (1,)), ((), ())), preferred_element_type=F32)


def add_log(a, b):
    top = jnp.maximum(a, b)
    return top + jnp.log(jnp.exp2(a - top) + jnp.exp2(b - top)) * LOG2E


def iota(shape, axis):
    return lax.broadcasted_iota(jnp.int32, shape, axis)


def kernel(
    q_hbm, k_hbm, v_hbm, order_hbm, att_ref, lse_ref, col_ref,
    qin, order_ref, kbuf, vbuf, qd, qb, hot, ex, m_s, l_s, f_s, ot, vt, cs, csr, lpart, lrecv, share,
    obuf, orecv, osum, load, send, recv,
):
    me = lax.axis_index("seq")
    z, y, c = me // 4, (me // 2) % 2, me % 2

    def device(dz, dy, dc):
        zz = lax.rem(z + dz + Z, Z)
        yy = 1 - y if dy else y
        cc = 1 - c if dc else c
        return {"seq": zz * 4 + yy * 2 + cc}

    barrier = pltpu.get_barrier_semaphore()
    partners = [(d, 0, 0) for d in (-3, -2, -1, 1, 2, 3)] + [(0, 0, 1), (0, 1, 0), (0, 1, 1)]
    for p in partners:
        pl.semaphore_signal(barrier, inc=1, device_id=device(*p), device_id_type=MESH)

    loads = [
        pltpu.make_async_copy(q_hbm, qin, load.at[0]),
        pltpu.make_async_copy(k_hbm, kbuf.at[pl.ds(0, ROWS)], load.at[1]),
        pltpu.make_async_copy(v_hbm, vbuf.at[pl.ds(0, ROWS)], load.at[2]),
        pltpu.make_async_copy(order_hbm, order_ref, load.at[3]),
    ]
    for cp in loads:
        cp.start()

    pending = []

    def remote(src, dst, index, target):
        return pltpu.make_async_remote_copy(
            src_ref=src, dst_ref=dst, send_sem=send.at[index], recv_sem=recv.at[index],
            device_id=target, device_id_type=MESH,
        )

    def push(*args):
        cp = remote(*args)
        cp.start()
        pending.append(cp)

    bufs = (kbuf, vbuf)

    def forward(a, rho):
        for dz, lo, rows in COPIES_FROM.get(rho, ()):
            push(
                bufs[a].at[pl.ds(slot(rho) * ROWS + lo, rows)],
                bufs[a].at[pl.ds(slot(rho - dz) * ROWS + lo, rows)],
                a * COPIES + NUMBER[rho, dz], device(dz, 0, 0),
            )

    def arrive(a, rho):
        for index, lo, rows in ARRIVALS[rho % Z]:
            here = bufs[a].at[pl.ds(slot(rho) * ROWS + lo, rows)]
            remote(here, here, a * COPIES + index, device(1, 0, 0)).wait_recv()
        forward(a, rho)

    for r in range(0, KEYS, 512):
        hot[r:r + 512, :] = jnp.where(
            iota((512, 128), 1) == (iota((512, 128), 0) + r) // BLOCK, 1.0, 0.0
        ).astype(BF16)
    row, lane, lane1 = iota((128, 128), 0), iota((128, 128), 1), iota((1, 128), 1)
    rho = jnp.zeros((128, 128), jnp.int32)
    for at, value in enumerate(ORDER):
        rho = jnp.where(row // 2 == at, value % Z, rho)
    index = 2 * (((z + rho) % Z) * 4 + y * 2 + c) + row % 2
    kr, qr = iota((ROWS, TILE), 0), iota((ROWS, TILE), 1) % ROWS
    tri = jnp.where((kr // BLOCK == qr // BLOCK) & (kr > qr), NEG, 0.0)
    half = (iota((1, TILE), 1) % ROWS) // BLOCK
    loads[3].wait()
    order = order_ref[...]
    key_block = jnp.sum(jnp.where(lane == index, order, 0), axis=1, keepdims=True)
    for g in range(4):
        yy = 1 - y if g // 2 else y
        cc = 1 - c if g % 2 else c
        first = 2 * (z * 4 + yy * 2 + cc)
        b0 = jnp.sum(jnp.where(lane1 == first, order, 0), axis=1, keepdims=True)
        b1 = jnp.sum(jnp.where(lane1 == first + 1, order, 0), axis=1, keepdims=True)
        query_block = jnp.where(half == 0, b0, b1)
        bad = (key_block > query_block) & (iota((128, TILE), 0) < 2 * Z)
        qb[g] = jnp.where(bad, NEG, 0.0).astype(BF16)
    loads[0].wait()
    for h in range(HEADS):
        part = qin[:, h * DIM:(h + 1) * DIM].astype(F32)
        qd[h // 2, :, (h % 2) * ROWS:(h % 2 + 1) * ROWS] = jnp.transpose(part).astype(BF16)
    loads[1].wait()
    loads[2].wait()

    def scores(ci, g):
        lo, n = CHUNKS[ci]
        for t in range(4 * g, 4 * g + 4):
            lhs = jnp.concatenate([kbuf[lo:lo + n, :], hot[lo:lo + n, :]], axis=1)
            rhs = jnp.concatenate([qd[t], qb[g]], axis=0)
            s = jnp.dot(lhs, rhs, preferred_element_type=F32)
            if ci == 0 and g == 0:
                s = jnp.concatenate([s[:ROWS] + tri, s[ROWS:]], axis=0)
            top = jnp.max(s, axis=0, keepdims=True) * SCALE
            p = jnp.exp2(s * SCALE - top)
            m_s[ci, t] = top
            l_s[ci, t] = jnp.sum(p, axis=0, keepdims=True)
            ex[t, lo:lo + n, :] = p.astype(BF16)

    def column(ci):
        lo, n = CHUNKS[ci]
        pick = iota((16, TILE), 0)
        total = jnp.zeros((16, n), F32)
        for t in range(DOT_TILES):
            f = f_s[ci, t]
            high = f.astype(BF16).astype(F32)
            w = jnp.where(pick == 0, high, jnp.where(pick == 1, f - high, 0.0)).astype(BF16)
            total = total + dot_nt(w, ex[t, lo:lo + n, :])
        total = total[0:1] + total[1:2]
        for b in range(n // ROWS):
            at = lo + b * ROWS
            rest = jnp.zeros((ROWS, 128), F32)
            for t in range(DOT_TILES, TILES):
                f = f_s[ci, t]
                for h in (0, 128):
                    rest = rest + ex[t, at:at + ROWS, h:h + 128].astype(F32) * f[:, h:h + 128]
            rest = jnp.sum(jnp.transpose(rest), axis=0, keepdims=True)
            cs[at // ROWS] = total[:, b * ROWS:(b + 1) * ROWS] + rest
        for rho in GROUPS[ci]:
            if rho:
                push(cs.at[slot(rho)], csr.at[slot(-rho)], SEM_COL + slot(-rho), device(rho % Z, 0, 0))

    def mix(t):
        total = None
        for ci, (lo, n) in enumerate(CHUNKS):
            o = jnp.dot(vt[:, lo:lo + n], ex[t, lo:lo + n, :], preferred_element_type=F32)
            o = o * jnp.exp2(m_s[ci, t] - lpart[t])
            total = o if total is None else total + o
        return total

    queries = [
        remote(qd.at[pl.ds(0, 4)], qd.at[pl.ds(4, 4)], SEM_Q, device(0, 0, 1)),
        remote(qd.at[pl.ds(0, 4)], qd.at[pl.ds(8, 4)], SEM_Q + 1, device(0, 1, 0)),
        remote(qd.at[pl.ds(8, 4)], qd.at[pl.ds(12, 4)], SEM_Q + 2, device(0, 0, 1)),
    ]
    pending.extend(queries)

    pl.semaphore_wait(barrier, len(partners))

    forward(0, 0)
    queries[1].start()
    queries[0].start()
    forward(1, 0)
    for what, *at in EVENTS:
        if what == "S":
            scores(*at)
        elif what == "Q":
            queries[at[0] - 1].wait_recv()
            if at[0] == 2:
                queries[2].start()
        else:
            arrive("KV".index(what), at[0])
            if at[0] != 8:
                arrive("KV".index(what), -at[0])

    for t in range(TILES):
        top = m_s[0, t]
        for ci in range(1, NC):
            top = jnp.maximum(top, m_s[ci, t])
        total = l_s[0, t] * jnp.exp2(m_s[0, t] - top)
        for ci in range(1, NC):
            total = total + l_s[ci, t] * jnp.exp2(m_s[ci, t] - top)
        lpart[t] = top + jnp.log(total) * LOG2E
    lses = [remote(lpart, lrecv.at[g - 1], SEM_LSE + g - 1, device(0, g // 2, g % 2)) for g in (3, 2, 1)]
    for cp in lses:
        cp.start()
    pending.extend(lses)
    for rho in V_LAST:
        arrive(1, rho)
        if rho != 8:
            arrive(1, -rho)
    for ci, (lo, n) in enumerate(CHUNKS):
        vt[:, lo:lo + n] = jnp.transpose(vbuf[lo:lo + n, :].astype(F32)).astype(BF16)

    def out_copy(kind, t):
        src = (obuf.at[t], obuf.at[4 + t], osum.at[t])[kind]
        return remote(src, orecv.at[4 * kind + t], SEM_OUT + 4 * kind + t, device(0, *((0, 1), (0, 1), (1, 0))[kind]))

    outs = [[out_copy(kind, t) for t in range(4)] for kind in range(3)]
    for t in range(4):
        obuf[t] = mix(12 + t).astype(BF16)
        outs[0][t].start()
    for t in range(4):
        ot[t] = mix(8 + t)
    lses[2].wait_recv()
    for t in range(4):
        a, b = lpart[8 + t], lrecv[0, 12 + t]
        two = add_log(a, b)
        outs[0][t].wait_recv()
        osum[t] = (ot[t] * jnp.exp2(a - two) + orecv[t].astype(F32) * jnp.exp2(b - two)).astype(BF16)
        outs[2][t].start()
    lses[1].wait_recv()
    lses[0].wait_recv()
    for t in range(TILES):
        g = t // 4
        parts = [lpart[t]] + [lrecv[o - 1, (o ^ g) * 4 + t % 4] for o in (1, 2, 3)]
        pair = add_log(parts[2], parts[3])
        lse = add_log(add_log(parts[0], parts[1]), pair)
        for ci in range(NC):
            f_s[ci, t] = jnp.exp2(m_s[ci, t] - lse)
        if t < 4:
            share[0, t] = jnp.exp2(parts[0] - lse)
            share[1, t] = jnp.exp2(parts[1] - lse)
            share[2, t] = jnp.exp2(pair - lse)
            for h in range(2):
                lse_ref[2 * t + h:2 * t + h + 1, :] = lse[:, h * ROWS:(h + 1) * ROWS] / LOG2E
    for ci in COLUMN_ORDER:
        column(ci)
    for t in range(4):
        obuf[4 + t] = mix(4 + t).astype(BF16)
        outs[1][t].start()
    for t in range(4):
        ot[t] = mix(t)
    for t in range(4):
        outs[1][t].wait_recv()
        outs[2][t].wait_recv()
        o = (
            ot[t] * share[0, t] + orecv[4 + t].astype(F32) * share[1, t] + orecv[8 + t].astype(F32) * share[2, t]
        )
        for h in range(2):
            at = (2 * t + h) * DIM
            att_ref[:, at:at + DIM] = jnp.transpose(o[:, h * ROWS:(h + 1) * ROWS]).astype(BF16)

    total = cs[0]
    for s in range(1, Z):
        remote(cs.at[s], csr.at[s], SEM_COL + s, device(1, 0, 0)).wait_recv()
        total = total + csr[s]
    col_ref[...] = total
    for cp in pending + outs[0] + outs[1] + outs[2]:
        cp.wait_send()


def finish(attention, row_lse, columns, attention_out, row_lse_out, columns_out):
    attention_out[...] = attention[...]
    row_lse_out[...] = row_lse[...]
    columns_out[...] = columns[...]


def local(queries, keys, values, block_order):
    vmem = pl.BlockSpec(memory_space=pltpu.VMEM)
    hbm = pl.BlockSpec(memory_space=pltpu.HBM)
    results = (
        jax.ShapeDtypeStruct((ROWS, HEADS * DIM), BF16),
        jax.ShapeDtypeStruct((HEADS, ROWS), F32),
        jax.ShapeDtypeStruct((1, ROWS), F32),
    )
    made = pl.pallas_call(
        kernel,
        out_shape=results,
        in_specs=[hbm] * 4,
        out_specs=(vmem,) * 3,
        scratch_shapes=[
            pltpu.VMEM((ROWS, HEADS * DIM), BF16),
            pltpu.VMEM((1, 128), jnp.int32),
            pltpu.VMEM((KEYS, DIM), BF16),
            pltpu.VMEM((KEYS, DIM), BF16),
            pltpu.VMEM((TILES, DIM, TILE), BF16),
            pltpu.VMEM((4, 128, TILE), BF16),
            pltpu.VMEM((KEYS, 128), BF16),
            pltpu.VMEM((TILES, KEYS, TILE), BF16),
            pltpu.VMEM((NC, TILES, 1, TILE), F32),
            pltpu.VMEM((NC, TILES, 1, TILE), F32),
            pltpu.VMEM((NC, TILES, 1, TILE), F32),
            pltpu.VMEM((4, DIM, TILE), F32),
            pltpu.VMEM((DIM, KEYS), BF16),
            pltpu.VMEM((Z, 1, ROWS), F32),
            pltpu.VMEM((Z, 1, ROWS), F32),
            pltpu.VMEM((TILES, 1, TILE), F32),
            pltpu.VMEM((3, TILES, 1, TILE), F32),
            pltpu.VMEM((3, 4, 1, TILE), F32),
            pltpu.VMEM((8, DIM, TILE), BF16),
            pltpu.VMEM((12, DIM, TILE), BF16),
            pltpu.VMEM((4, DIM, TILE), BF16),
            pltpu.SemaphoreType.DMA((4,)),
            pltpu.SemaphoreType.DMA((SEMS,)),
            pltpu.SemaphoreType.DMA((SEMS,)),
        ],
        compiler_params=pltpu.CompilerParams(
            collective_id=0, has_side_effects=True, vmem_limit_bytes=63 * 2**20
        ),
        cost_estimate=pl.CostEstimate(flops=9 * 10**9, bytes_accessed=10**6, transcendentals=9 * 10**6),
    )(queries, keys, values, block_order.reshape(1, -1))
    attention, row_lse, columns = pl.pallas_call(
        finish,
        out_shape=results,
        in_specs=[vmem] * 3,
        out_specs=(vmem,) * 3,
        compiler_params=pltpu.CompilerParams(vmem_limit_bytes=63 * 2**20),
        cost_estimate=pl.CostEstimate(flops=0, bytes_accessed=10**6, transcendentals=0),
    )(*made)
    return attention, row_lse, columns.reshape(ROWS)


def solution(mesh):
    placed = (P("seq", "kv"), P("seq", "kv"), P("seq", "kv"), P())
    return jax.shard_map(
        local,
        mesh=mesh,
        in_specs=placed,
        out_specs=(P("seq", "kv"), P("kv", "seq"), P(("kv", "seq"))),
        check_vma=False,
    )
```

```python
import functools
import math

import jax
import jax.numpy as jnp
from jax import lax
from jax.experimental import pallas as pl
from jax.experimental.pallas import tpu as pltpu
from jax.sharding import PartitionSpec as P

MESH = pl.DeviceIdType.MESH
F32, BF16 = jnp.float32, jnp.bfloat16
BLOCK = 64
ROWS = 128
DIM = 128
HEADS = 8
Z = 16
TILE = 256
TILES = 16
NEG = -1e30
LOG2E = math.log2(math.e)
SCALE = LOG2E / math.sqrt(DIM)
KEYS = Z * ROWS
GROUPS = [(0, 1, -1), (3, -3), (2, -2, 4, -4), (6, -6), (5, -5), (7, -7, 8)]
ORDER = [rho for group in GROUPS for rho in group]
CHUNKS = []
for group in GROUPS:
    CHUNKS.append((sum(n for _, n in CHUNKS), ROWS * len(group)))
NC = len(CHUNKS)
PLACE = {rho % Z: at for at, rho in enumerate(ORDER)}


def slot(rho):
    return PLACE[rho % Z]


COPIES_FROM = {
    0: [(3, 0, ROWS), (-3, 0, ROWS), (1, 0, ROWS), (-1, 0, ROWS)],
    -3: [(3, 0, ROWS), (1, 0, ROWS), (-1, 0, ROWS)],
    3: [(-3, 0, ROWS), (-1, 0, ROWS), (1, 0, ROWS)],
    -6: [(2, 0, 64), (1, 0, ROWS), (-1, 0, ROWS)],
    6: [(-2, 64, 64), (-1, 0, ROWS), (1, 0, ROWS)],
}
NUMBER, ARRIVALS = {}, {}
for rho, copies in COPIES_FROM.items():
    for dz, lo, rows in copies:
        NUMBER[rho, dz] = len(NUMBER)
        ARRIVALS.setdefault((rho - dz) % Z, []).append((NUMBER[rho, dz], lo, rows))
COPIES = len(NUMBER)
SEM_COL = 2 * COPIES
SEM_Q = SEM_COL + Z
SEM_LSE = SEM_Q + 3
SEM_OUT = SEM_LSE + 3
SEMS = SEM_OUT + 12

EVENTS = [
    ("K", 3), ("K", 1), ("Q", 1), ("S", 0, 0), ("S", 0, 1), ("S", 1, 0), ("S", 1, 1),
    ("V", 3), ("Q", 2), ("S", 0, 2), ("S", 1, 2), ("K", 6), ("V", 1), ("Q", 3), ("S", 0, 3), ("S", 1, 3),
    ("K", 2), ("K", 4), ("S", 2, 0), ("S", 2, 1), ("S", 2, 2), ("S", 2, 3),
    ("S", 3, 0), ("S", 3, 1), ("S", 3, 2), ("S", 3, 3),
    ("V", 6), ("K", 5), ("S", 4, 0), ("S", 4, 1), ("S", 4, 2), ("S", 4, 3),
    ("K", 7), ("K", 8), ("S", 5, 0), ("S", 5, 1), ("S", 5, 2), ("S", 5, 3),
]

DOT_TILES = 8
V_LAST = (2, 4, 5, 7, 8)
COLUMN_ORDER = (5, 3, 4, 2, 1, 0)


def dot_nt(a, b):
    return lax.dot_general(a, b, (((1,), (1,)), ((), ())), preferred_element_type=F32)


def add_log(a, b):
    top = jnp.maximum(a, b)
    return top + jnp.log(jnp.exp2(a - top) + jnp.exp2(b - top)) * LOG2E


def iota(shape, axis):
    return lax.broadcasted_iota(jnp.int32, shape, axis)


def kernel(
    q_hbm, k_hbm, v_hbm, order_hbm, att_ref, lse_ref, col_ref,
    qin, order_ref, kbuf, vbuf, qd, qb, hot, ex, m_s, l_s, f_s, ot, vt, cs, csr, lpart, lrecv, share,
    obuf, orecv, osum, load, send, recv,
):
    me = lax.axis_index("seq")
    z, y, c = me // 4, (me // 2) % 2, me % 2

    def device(dz, dy, dc):
        zz = lax.rem(z + dz + Z, Z)
        yy = 1 - y if dy else y
        cc = 1 - c if dc else c
        return {"seq": zz * 4 + yy * 2 + cc}

    barrier = pltpu.get_barrier_semaphore()
    partners = [(d, 0, 0) for d in (-3, -2, -1, 1, 2, 3)] + [(0, 0, 1), (0, 1, 0), (0, 1, 1)]
    for p in partners:
        pl.semaphore_signal(barrier, inc=1, device_id=device(*p), device_id_type=MESH)

    loads = [
        pltpu.make_async_copy(q_hbm, qin, load.at[0]),
        pltpu.make_async_copy(k_hbm, kbuf.at[pl.ds(0, ROWS)], load.at[1]),
        pltpu.make_async_copy(v_hbm, vbuf.at[pl.ds(0, ROWS)], load.at[2]),
        pltpu.make_async_copy(order_hbm, order_ref, load.at[3]),
    ]
    for cp in loads:
        cp.start()

    pending = []

    def remote(src, dst, index, target):
        return pltpu.make_async_remote_copy(
            src_ref=src, dst_ref=dst, send_sem=send.at[index], recv_sem=recv.at[index],
            device_id=target, device_id_type=MESH,
        )

    def push(*args):
        cp = remote(*args)
        cp.start()
        pending.append(cp)

    bufs = (kbuf, vbuf)

    def forward(a, rho, steps=(1, 2, 3)):
        for dz, lo, rows in COPIES_FROM.get(rho, ()):
            if abs(dz) not in steps:
                continue
            push(
                bufs[a].at[pl.ds(slot(rho) * ROWS + lo, rows)],
                bufs[a].at[pl.ds(slot(rho - dz) * ROWS + lo, rows)],
                a * COPIES + NUMBER[rho, dz], device(dz, 0, 0),
            )

    def arrive(a, rho):
        for index, lo, rows in ARRIVALS[rho % Z]:
            here = bufs[a].at[pl.ds(slot(rho) * ROWS + lo, rows)]
            remote(here, here, a * COPIES + index, device(1, 0, 0)).wait_recv()
        forward(a, rho)

    for r in range(0, KEYS, 512):
        hot[r:r + 512, :] = jnp.where(
            iota((512, 128), 1) == (iota((512, 128), 0) + r) // BLOCK, 1.0, 0.0
        ).astype(BF16)
    row, lane, lane1 = iota((128, 128), 0), iota((128, 128), 1), iota((1, 128), 1)
    rho = jnp.zeros((128, 128), jnp.int32)
    for at, value in enumerate(ORDER):
        rho = jnp.where(row // 2 == at, value % Z, rho)
    index = 2 * (((z + rho) % Z) * 4 + y * 2 + c) + row % 2
    kr, qr = iota((ROWS, TILE), 0), iota((ROWS, TILE), 1) % ROWS
    tri = jnp.where((kr // BLOCK == qr // BLOCK) & (kr > qr), NEG, 0.0)
    half = (iota((1, TILE), 1) % ROWS) // BLOCK
    loads[3].wait()
    order = order_ref[...]
    key_block = jnp.sum(jnp.where(lane == index, order, 0), axis=1, keepdims=True)
    for g in range(4):
        yy = 1 - y if g // 2 else y
        cc = 1 - c if g % 2 else c
        first = 2 * (z * 4 + yy * 2 + cc)
        b0 = jnp.sum(jnp.where(lane1 == first, order, 0), axis=1, keepdims=True)
        b1 = jnp.sum(jnp.where(lane1 == first + 1, order, 0), axis=1, keepdims=True)
        query_block = jnp.where(half == 0, b0, b1)
        bad = (key_block > query_block) & (iota((128, TILE), 0) < 2 * Z)
        qb[g] = jnp.where(bad, NEG, 0.0).astype(BF16)
    loads[0].wait()
    for h in range(HEADS):
        part = qin[:, h * DIM:(h + 1) * DIM].astype(F32)
        qd[h // 2, :, (h % 2) * ROWS:(h % 2 + 1) * ROWS] = jnp.transpose(part).astype(BF16)
    loads[1].wait()
    loads[2].wait()

    def scores(ci, g):
        lo, n = CHUNKS[ci]
        for t in range(4 * g, 4 * g + 4):
            lhs = jnp.concatenate([kbuf[lo:lo + n, :], hot[lo:lo + n, :]], axis=1)
            rhs = jnp.concatenate([qd[t], qb[g]], axis=0)
            s = jnp.dot(lhs, rhs, preferred_element_type=F32)
            if ci == 0 and g == 0:
                s = jnp.concatenate([s[:ROWS] + tri, s[ROWS:]], axis=0)
            top = jnp.max(s, axis=0, keepdims=True) * SCALE
            p = jnp.exp2(s * SCALE - top)
            m_s[ci, t] = top
            l_s[ci, t] = jnp.sum(p, axis=0, keepdims=True)
            ex[t, lo:lo + n, :] = p.astype(BF16)

    def column(ci):
        lo, n = CHUNKS[ci]
        pick = iota((16, TILE), 0)
        total = jnp.zeros((16, n), F32)
        for t in range(DOT_TILES):
            f = f_s[ci, t]
            high = f.astype(BF16).astype(F32)
            w = jnp.where(pick == 0, high, jnp.where(pick == 1, f - high, 0.0)).astype(BF16)
            total = total + dot_nt(w, ex[t, lo:lo + n, :])
        total = total[0:1] + total[1:2]
        for b in range(n // ROWS):
            at = lo + b * ROWS
            rest = jnp.zeros((ROWS, 128), F32)
            for t in range(DOT_TILES, TILES):
                f = f_s[ci, t]
                for h in (0, 128):
                    rest = rest + ex[t, at:at + ROWS, h:h + 128].astype(F32) * f[:, h:h + 128]
            rest = jnp.sum(jnp.transpose(rest), axis=0, keepdims=True)
            cs[at // ROWS] = total[:, b * ROWS:(b + 1) * ROWS] + rest
        for rho in GROUPS[ci]:
            if rho:
                push(cs.at[slot(rho)], csr.at[slot(-rho)], SEM_COL + slot(-rho), device(rho % Z, 0, 0))

    def mix(t):
        total = None
        for ci, (lo, n) in enumerate(CHUNKS):
            o = jnp.dot(vt[:, lo:lo + n], ex[t, lo:lo + n, :], preferred_element_type=F32)
            o = o * jnp.exp2(m_s[ci, t] - lpart[t])
            total = o if total is None else total + o
        return total

    queries = [
        remote(qd.at[pl.ds(0, 4)], qd.at[pl.ds(4, 4)], SEM_Q, device(0, 0, 1)),
        remote(qd.at[pl.ds(0, 4)], qd.at[pl.ds(8, 4)], SEM_Q + 1, device(0, 1, 0)),
        remote(qd.at[pl.ds(8, 4)], qd.at[pl.ds(12, 4)], SEM_Q + 2, device(0, 0, 1)),
    ]
    pending.extend(queries)

    pl.semaphore_wait(barrier, len(partners))

    forward(0, 0, (3,))
    queries[1].start()
    queries[0].start()
    forward(1, 0, (3,))
    forward(0, 0, (1,))
    forward(1, 0, (1,))
    for what, *at in EVENTS:
        if what == "S":
            scores(*at)
        elif what == "Q":
            queries[at[0] - 1].wait_recv()
            if at[0] == 2:
                queries[2].start()
        else:
            arrive("KV".index(what), at[0])
            if at[0] != 8:
                arrive("KV".index(what), -at[0])

    for t in range(TILES):
        top = m_s[0, t]
        for ci in range(1, NC):
            top = jnp.maximum(top, m_s[ci, t])
        total = l_s[0, t] * jnp.exp2(m_s[0, t] - top)
        for ci in range(1, NC):
            total = total + l_s[ci, t] * jnp.exp2(m_s[ci, t] - top)
        lpart[t] = top + jnp.log(total) * LOG2E
    lses = [remote(lpart, lrecv.at[g - 1], SEM_LSE + g - 1, device(0, g // 2, g % 2)) for g in (3, 2, 1)]
    for cp in lses:
        cp.start()
    pending.extend(lses)
    for rho in V_LAST:
        arrive(1, rho)
        if rho != 8:
            arrive(1, -rho)
    for ci, (lo, n) in enumerate(CHUNKS):
        vt[:, lo:lo + n] = jnp.transpose(vbuf[lo:lo + n, :].astype(F32)).astype(BF16)

    def out_copy(kind, t):
        src = (obuf.at[t], obuf.at[4 + t], osum.at[t])[kind]
        return remote(src, orecv.at[4 * kind + t], SEM_OUT + 4 * kind + t, device(0, *((0, 1), (0, 1), (1, 0))[kind]))

    outs = [[out_copy(kind, t) for t in range(4)] for kind in range(3)]
    for t in range(4):
        obuf[t] = mix(12 + t).astype(BF16)
        outs[0][t].start()
    for t in range(4):
        ot[t] = mix(8 + t)
    lses[2].wait_recv()
    for t in range(4):
        a, b = lpart[8 + t], lrecv[0, 12 + t]
        two = add_log(a, b)
        outs[0][t].wait_recv()
        osum[t] = (ot[t] * jnp.exp2(a - two) + orecv[t].astype(F32) * jnp.exp2(b - two)).astype(BF16)
        outs[2][t].start()
    lses[1].wait_recv()
    lses[0].wait_recv()
    for t in range(TILES):
        g = t // 4
        parts = [lpart[t]] + [lrecv[o - 1, (o ^ g) * 4 + t % 4] for o in (1, 2, 3)]
        pair = add_log(parts[2], parts[3])
        lse = add_log(add_log(parts[0], parts[1]), pair)
        for ci in range(NC):
            f_s[ci, t] = jnp.exp2(m_s[ci, t] - lse)
        if t < 4:
            share[0, t] = jnp.exp2(parts[0] - lse)
            share[1, t] = jnp.exp2(parts[1] - lse)
            share[2, t] = jnp.exp2(pair - lse)
            for h in range(2):
                lse_ref[2 * t + h:2 * t + h + 1, :] = lse[:, h * ROWS:(h + 1) * ROWS] / LOG2E
    for ci in COLUMN_ORDER:
        column(ci)
    for t in range(4):
        obuf[4 + t] = mix(4 + t).astype(BF16)
        outs[1][t].start()
    for t in range(4):
        ot[t] = mix(t)
    for t in range(4):
        outs[1][t].wait_recv()
        outs[2][t].wait_recv()
        o = (
            ot[t] * share[0, t] + orecv[4 + t].astype(F32) * share[1, t] + orecv[8 + t].astype(F32) * share[2, t]
        )
        for h in range(2):
            at = (2 * t + h) * DIM
            att_ref[:, at:at + DIM] = jnp.transpose(o[:, h * ROWS:(h + 1) * ROWS]).astype(BF16)

    total = cs[0]
    for s in range(1, Z):
        remote(cs.at[s], csr.at[s], SEM_COL + s, device(1, 0, 0)).wait_recv()
        total = total + csr[s]
    col_ref[...] = total
    for cp in pending + outs[0] + outs[1] + outs[2]:
        cp.wait_send()


def finish(attention, row_lse, columns, attention_out, row_lse_out, columns_out):
    attention_out[...] = attention[...]
    row_lse_out[...] = row_lse[...]
    columns_out[...] = columns[...]


def local(queries, keys, values, block_order):
    vmem = pl.BlockSpec(memory_space=pltpu.VMEM)
    hbm = pl.BlockSpec(memory_space=pltpu.HBM)
    results = (
        jax.ShapeDtypeStruct((ROWS, HEADS * DIM), BF16),
        jax.ShapeDtypeStruct((HEADS, ROWS), F32),
        jax.ShapeDtypeStruct((1, ROWS), F32),
    )
    made = pl.pallas_call(
        kernel,
        out_shape=results,
        in_specs=[hbm] * 4,
        out_specs=(vmem,) * 3,
        scratch_shapes=[
            pltpu.VMEM((ROWS, HEADS * DIM), BF16),
            pltpu.VMEM((1, 128), jnp.int32),
            pltpu.VMEM((KEYS, DIM), BF16),
            pltpu.VMEM((KEYS, DIM), BF16),
            pltpu.VMEM((TILES, DIM, TILE), BF16),
            pltpu.VMEM((4, 128, TILE), BF16),
            pltpu.VMEM((KEYS, 128), BF16),
            pltpu.VMEM((TILES, KEYS, TILE), BF16),
            pltpu.VMEM((NC, TILES, 1, TILE), F32),
            pltpu.VMEM((NC, TILES, 1, TILE), F32),
            pltpu.VMEM((NC, TILES, 1, TILE), F32),
            pltpu.VMEM((4, DIM, TILE), F32),
            pltpu.VMEM((DIM, KEYS), BF16),
            pltpu.VMEM((Z, 1, ROWS), F32),
            pltpu.VMEM((Z, 1, ROWS), F32),
            pltpu.VMEM((TILES, 1, TILE), F32),
            pltpu.VMEM((3, TILES, 1, TILE), F32),
            pltpu.VMEM((3, 4, 1, TILE), F32),
            pltpu.VMEM((8, DIM, TILE), BF16),
            pltpu.VMEM((12, DIM, TILE), BF16),
            pltpu.VMEM((4, DIM, TILE), BF16),
            pltpu.SemaphoreType.DMA((4,)),
            pltpu.SemaphoreType.DMA((SEMS,)),
            pltpu.SemaphoreType.DMA((SEMS,)),
        ],
        compiler_params=pltpu.CompilerParams(
            collective_id=0, has_side_effects=True, vmem_limit_bytes=63 * 2**20
        ),
        cost_estimate=pl.CostEstimate(flops=9 * 10**9, bytes_accessed=10**6, transcendentals=9 * 10**6),
    )(queries, keys, values, block_order.reshape(1, -1))
    attention, row_lse, columns = pl.pallas_call(
        finish,
        out_shape=results,
        in_specs=[vmem] * 3,
        out_specs=(vmem,) * 3,
        compiler_params=pltpu.CompilerParams(vmem_limit_bytes=63 * 2**20),
        cost_estimate=pl.CostEstimate(flops=0, bytes_accessed=10**6, transcendentals=0),
    )(*made)
    return attention, row_lse, columns.reshape(ROWS)


def solution(mesh):
    placed = (P("seq", "kv"), P("seq", "kv"), P("seq", "kv"), P())
    return jax.shard_map(
        local,
        mesh=mesh,
        in_specs=placed,
        out_specs=(P("seq", "kv"), P("kv", "seq"), P(("kv", "seq"))),
        check_vma=False,
    )
```
